256 devices in a mesh: expert: 32 (over x_hi, z, core), blk: 8 (over x_lo, y).
Axes of the slice: x: 4 (x_hi: 2, x_lo: 2; x = x_hi * 2 + x_lo), y: 4, z: 8, core: 2. Of those that a mesh axis runs over, the one named last changes fastest.
Arguments:
- tokens: bfloat16 [8192, 7168], P('expert', 'blk'), may hold values from -6 to 6
- cotangent: bfloat16 [8192, 7168], P('expert', 'blk'), may hold values from -6 to 6
- expert_ids: int32 [8192, 8], P('expert'), may hold values from 0 to 255, as said below
- gate_fixed: int32 [8192, 8], P('expert'), may hold values from 4096 to 65535
- w_gate: bfloat16 [32, 7168, 1024], P('expert', 'blk'), may hold values from -0.0625 to 0.0625
- w_up: bfloat16 [32, 7168, 1024], P('expert', 'blk'), may hold values from -0.0625 to 0.0625
- w_down: bfloat16 [32, 1024, 7168], P('expert', None, 'blk'), may hold values from -0.1875 to 0.1875
Outputs:
- layer_out: bfloat16 [8192, 7168], P('expert', 'blk')
- grad_gate: bfloat16 [32, 7168, 1024], P('expert', 'blk')
- grad_up: bfloat16 [32, 7168, 1024], P('expert', 'blk')
- grad_down: bfloat16 [32, 1024, 7168], P('expert', None, 'blk')
- loads: int32 [256], replicated
The draws below stay inside these ranges and needn't reach their ends.
Inputs may be any that keep to these rules, and one draw needn't show every extreme that they name: `expert_ids`: each token names 8 different experts. Among the tokens of one index of expert no expert is named by more than 16 tokens, and some expert below 32 is named by exactly 16 tokens of every index.
All inputs are finite; a program needn't handle non-finite values.
Results may differ from the reference program's by a relative error of at most 0.029.
Values may be sent and summed in bfloat16 or wider, within the bound.
No kernel may reach another device: no remote copies, remote signals or barrier semaphores. Data moves between devices by JAX's collectives and lax.ppermute only.
A program may use at most 64 MiB of HBM per device.

```python
import jax
import jax.numpy as jnp
from jax import lax

D = 7168
EXPERTS_ALL = 256
TOPK = 8
FF = 1024
TOK = 256
EXPERTS = 32
TOKENS = 8192
CAP = 16
N_EXPERT = 32
N_BLK = 8


def draw_expert_ids(key, part):
    key = jax.random.fold_in(key, 11)
    hottest = jax.random.randint(jax.random.fold_in(key, 1), (), 0, EXPERTS)
    base = TOK * TOPK // EXPERTS_ALL

    def one_source(block_key):
        order_key, shift_key = jax.random.split(block_key)
        rest = jax.random.permutation(order_key, EXPERTS_ALL - 1).astype(jnp.int32) + 1
        order = jnp.concatenate([jnp.zeros((1,), jnp.int32), rest])
        order = (order + hottest) % EXPERTS_ALL
        shifts = jax.random.randint(shift_key, (EXPERTS_ALL // 2,), 0, base + 1)
        shifts = shifts.at[0].set(base)
        counts = jnp.stack([base + shifts, base - shifts], axis=1).reshape(-1)
        ends = jnp.cumsum(counts)
        positions = jnp.arange(TOK * TOPK, dtype=jnp.int32)
        rank_of = jnp.sum((positions[:, None] >= ends[None, :]).astype(jnp.int32), axis=1)
        sequence = order[rank_of]
        return sequence.reshape(TOPK, TOK).T
    source_keys = jax.random.split(jax.random.fold_in(key, 2), N_EXPERT)
    blocks = jax.vmap(one_source)(source_keys)
    return blocks.reshape(TOKENS, TOPK).astype(jnp.int32)


def with_ends(entries, rng, low, top_value):
    dims = entries.shape
    index_at = [jax.random.randint(jax.random.fold_in(rng, axis), (), 0, dims[axis]) for axis in range(len(dims))]
    entries = entries.at[tuple(index_at)].set(low)
    longest = dims.index(max(dims))
    index_at[longest] = (index_at[longest] + 1) % dims[longest]
    return entries.at[tuple(index_at)].set(top_value)


def block_levels(own_key, shape, cuts, least, high):
    factor_of = 1.0
    for position, blocks in cuts:
        heights = jax.random.uniform(jax.random.fold_in(jax.random.fold_in(own_key, 6), position), (blocks,), jnp.float32, least / len(cuts), high / len(cuts))
        factor_of = factor_of * jnp.repeat(jnp.exp(heights), shape[position] // blocks).reshape((-1,) + (1,) * (len(shape) - 1 - position))
    return factor_of


def noise(stream_key, extent, width, most, cuts=(), held_as=jnp.bfloat16):
    values = jax.random.normal(stream_key, extent, jnp.float32) * width
    if len(cuts) > 0:
        values = block_levels(stream_key, extent, cuts, -0.22, 0.18) * values
    return jnp.clip(values, min=-most, max=most).astype(held_as)


def setup_inputs(seed: int = 0) -> dict:
    seeds = jax.random.split(jax.random.key(seed), 8)
    return {
        "tokens": noise(seeds[0], (TOKENS, D), 1.0, 6.0, ((0, 32), (1, 8))),
        "cotangent": noise(seeds[1], (TOKENS, D), 0.5, 6.0, ((0, 32), (1, 8))),
        "expert_ids": draw_expert_ids(jax.random.fold_in(seeds[7], 71), 0),
        "gate_fixed": with_ends(jax.random.randint(seeds[3], (TOKENS, TOPK), 4096, 65536), jax.random.fold_in(seeds[3], 1), 4096, 65535).astype(jnp.int32),
        "w_gate": noise(seeds[4], (EXPERTS, D, FF), D ** -0.5, 0.0625, ((0, 32), (1, 8))),
        "w_up": noise(seeds[5], (EXPERTS, D, FF), D ** -0.5, 0.0625, ((0, 32), (1, 8))),
        "w_down": noise(seeds[6], (EXPERTS, FF, D), FF ** -0.5, 0.1875, ((0, 32), (2, 8))),
    }


def rounded_blocks(parts):
    parts = parts.astype(jnp.bfloat16)
    parts = lax.optimization_barrier(parts)
    return jnp.sum(parts.astype(jnp.float32), axis=0)


def expert_pass(tokens, cotangent, slot_token, slot_gate, slot_live, gate_slab, up_slab, down_slab):
    slot_rows = slot_token.shape[0]
    block_cols = D // N_BLK
    picked = tokens[slot_token]
    routed_x = jnp.where(slot_live[:, None] > 0, picked, jnp.zeros_like(picked))
    routed_cot = (slot_gate[:, None] * cotangent[slot_token].astype(jnp.float32)).astype(jnp.bfloat16)
    x_blocks = routed_x.reshape(slot_rows, N_BLK, block_cols).astype(jnp.float32)
    gate_parts = jnp.einsum("rjd,jdf->jrf", x_blocks, gate_slab.reshape(N_BLK, block_cols, FF).astype(jnp.float32))
    up_parts = jnp.einsum("rjd,jdf->jrf", x_blocks, up_slab.reshape(N_BLK, block_cols, FF).astype(jnp.float32))
    gate_pre = rounded_blocks(gate_parts)
    up_pre = rounded_blocks(up_parts)
    sigma = jax.nn.sigmoid(gate_pre)
    hidden = (gate_pre * sigma * up_pre).astype(jnp.bfloat16)
    expert_out = jnp.dot(hidden, down_slab, preferred_element_type=jnp.float32).astype(jnp.bfloat16)
    cot_blocks = routed_cot.reshape(slot_rows, N_BLK, block_cols).astype(jnp.float32)
    back_parts = jnp.einsum("rjd,fjd->jrf", cot_blocks, down_slab.reshape(FF, N_BLK, block_cols).astype(jnp.float32))
    d_hidden = rounded_blocks(back_parts)
    d_gate = (d_hidden * up_pre * sigma * (1.0 + gate_pre * (1.0 - sigma))).astype(jnp.bfloat16)
    d_up = (d_hidden * gate_pre * sigma).astype(jnp.bfloat16)
    grad_down = jnp.dot(hidden.T, routed_cot, preferred_element_type=jnp.float32).astype(jnp.bfloat16)
    grad_gate = jnp.dot(routed_x.T, d_gate, preferred_element_type=jnp.float32).astype(jnp.bfloat16)
    grad_up = jnp.dot(routed_x.T, d_up, preferred_element_type=jnp.float32).astype(jnp.bfloat16)
    return expert_out, grad_gate, grad_up, grad_down


def reference(tokens, cotangent, expert_ids, gate_fixed, w_gate, w_up, w_down):
    gate_values = gate_fixed.astype(jnp.float32) * (1.0 / 65536.0)
    source_ids = expert_ids.reshape(N_EXPERT, TOK * TOPK)
    onehot = (source_ids[:, :, None] == jnp.arange(EXPERTS, dtype=jnp.int32)[None, None, :]).astype(jnp.int32)
    rank_in = jnp.sum((jnp.cumsum(onehot, axis=1) - onehot) * onehot, axis=2)
    inside = source_ids < EXPERTS
    source = jnp.arange(N_EXPERT, dtype=jnp.int32)[:, None]
    total_slots = EXPERTS * N_EXPERT * CAP
    slot_index = jnp.where(inside, source_ids * (N_EXPERT * CAP) + source * CAP + rank_in, total_slots)
    slot_index = slot_index.reshape(-1).astype(jnp.int32)
    token_index = (jnp.arange(TOKENS * TOPK, dtype=jnp.int32) // TOPK).astype(jnp.int32)
    slot_token = jnp.zeros((total_slots + 1,), jnp.int32).at[slot_index].set(token_index)[:total_slots]
    slot_gate = jnp.zeros((total_slots + 1,), jnp.float32).at[slot_index].set(gate_values.reshape(-1))[:total_slots]
    slot_live = jnp.zeros((total_slots + 1,), jnp.float32).at[slot_index].set(1.0)[:total_slots]
    slot_token = slot_token.reshape(EXPERTS, N_EXPERT * CAP)
    slot_gate = slot_gate.reshape(EXPERTS, N_EXPERT * CAP)
    slot_live = slot_live.reshape(EXPERTS, N_EXPERT * CAP)

    def one_expert(pieces):
        return expert_pass(tokens, cotangent, *pieces)

    expert_out, grad_gate, grad_up, grad_down = lax.map(one_expert, (slot_token, slot_gate, slot_live, w_gate, w_up, w_down))
    weighted = slot_gate.reshape(-1)[:, None] * expert_out.reshape(-1, D).astype(jnp.float32)
    layer_out = jnp.zeros((TOKENS, D), jnp.float32).at[slot_token.reshape(-1)].add(weighted).astype(jnp.bfloat16)
    loads = jnp.zeros((EXPERTS_ALL,), jnp.int32).at[expert_ids.reshape(-1)].add(jnp.ones((TOKENS * TOPK,), jnp.int32))
    return layer_out, grad_gate, grad_up, grad_down, loads
```

```python
import jax
import jax.numpy as jnp
from jax import lax
from jax.experimental import pallas as pl
from jax.experimental.pallas import tpu as pltpu
from jax.sharding import PartitionSpec as P

EXPERTS_ALL = 256
TOPK = 8
CAP = 16
N_Y = 4
TILE = 256
F32 = jnp.float32
BF16 = jnp.bfloat16
MIB = 1024 * 1024
SMALL = 16 * MIB
LARGE = 58 * MIB
COUNT_LANES = 128


def iota(shape, dim):
    return lax.broadcasted_iota(jnp.int32, shape, dim)


def dot(left, right, dims):
    return lax.dot_general(left, right, (dims, ((), ())), preferred_element_type=F32)


def matmul(left, right):
    return jnp.dot(left, right, preferred_element_type=F32)


def rows_of(order_ref, d, chunk):
    return pl.ds(pl.multiple_of(order_ref[d] * chunk, chunk), chunk)


def columns_of(i):
    return pl.ds(pl.multiple_of(i * TILE, TILE), TILE)


def whole(array):
    zeros = (0,) * len(array.shape)
    return pl.BlockSpec(array.shape, lambda i: zeros)


def call(kernel, outs, *args, ordered=False, stay=(), limit=SMALL, flops=0, traffic=0, **options):
    outs = [jax.ShapeDtypeStruct(s, t) for s, t in outs]
    in_specs = [whole(a) for a in args]
    if ordered:
        in_specs[0] = pl.BlockSpec(memory_space=pltpu.SMEM)
    for i in stay:
        in_specs[i] = pl.BlockSpec(memory_space=pltpu.HBM)
    settings = dict(grid=(1,), in_specs=in_specs, out_specs=[whole(o) for o in outs])
    settings.update(options)
    return pl.pallas_call(
        kernel,
        out_shape=outs,
        compiler_params=pltpu.CompilerParams(vmem_limit_bytes=limit),
        cost_estimate=pl.CostEstimate(flops=flops, bytes_accessed=traffic, transcendentals=0),
        name=kernel.__name__,
        **settings,
    )(*args)


def ones_where(condition):
    return condition.astype(F32).astype(BF16)


def spread_of(slots, experts):
    return ones_where((iota((slots, experts), 0) // CAP) == iota((slots, experts), 1))


def slots_of(ids_ref, slots):
    rows = ids_ref.shape[1]
    experts = slots // CAP
    line = iota((experts, rows), 0)
    picked = jnp.zeros((experts, rows), F32)
    for k in range(TOPK):
        picked = jnp.where(ids_ref[k : k + 1, :] == line, 1.0, picked)
    rank = matmul(picked.astype(BF16), ones_where(iota((rows, rows), 0) < iota((rows, rows), 1)))
    key = jnp.where(picked > 0.5, rank, -1.0).astype(BF16)
    slot_rank = (iota((slots, rows), 0) % CAP).astype(F32)
    return (matmul(spread_of(slots, experts), key) == slot_rank).astype(F32)


def route(ids_ref, tok_ref, rx_ref):
    sel = slots_of(ids_ref, rx_ref.shape[0]).astype(BF16)
    rx_ref[...] = matmul(sel, tok_ref[...]).astype(BF16)


def route_back(ids_ref, gate_ref, cot_ref, rc_ref, gate_hi_ref, gate_lo_ref):
    rows, cols = cot_ref.shape
    slots = rc_ref.shape[0]
    experts = slots // CAP
    line = iota((experts, rows), 0)
    gate = jnp.zeros((experts, rows), jnp.int32)
    for k in range(TOPK):
        gate = jnp.where(ids_ref[k : k + 1, :] == line, gate_ref[k : k + 1, :], gate)
    spread = spread_of(slots, experts)
    select = slots_of(ids_ref, slots)
    hi = matmul(spread, (gate // 256).astype(F32).astype(BF16)) * select
    lo = matmul(spread, (gate % 256).astype(F32).astype(BF16)) * select
    slot_gate = jnp.sum(hi * 256.0 + lo, axis=1, keepdims=True) * (1.0 / 65536.0)
    rc_ref[:, :cols] = (slot_gate * matmul(select.astype(BF16), cot_ref[...])).astype(BF16)
    gate_hi_ref[...] = hi.T.astype(BF16)
    gate_lo_ref[...] = lo.T.astype(BF16)
    every = iota((EXPERTS_ALL, rows), 0)
    hits = jnp.zeros((EXPERTS_ALL, rows), F32)
    for k in range(TOPK):
        hits = hits + jnp.where(ids_ref[k : k + 1, :] == every, 1.0, 0.0)
    counts = dot(jnp.ones((CAP, rows), BF16), hits.astype(BF16), ((1,), (1,)))
    line = iota((CAP, COUNT_LANES), 0)
    block = jnp.where(line == 0, counts[:, :COUNT_LANES], jnp.where(line == 1, counts[:, COUNT_LANES:], 0.0))
    block = block.astype(BF16)
    for e in range(experts):
        rc_ref[e * CAP : (e + 1) * CAP, cols:] = block


def turn(order_ref, x_ref, out_ref, held):
    chunk = x_ref.shape[0] // order_ref.shape[0]
    for d in range(order_ref.shape[0]):
        held[d * chunk : (d + 1) * chunk, :] = x_ref[rows_of(order_ref, d, chunk), :]
    out_ref[...] = held[...].T


def in_order(order_ref, x_ref, held):
    @pl.when(pl.program_id(0) == 0)
    def _():
        n = order_ref.shape[0]
        chunk = x_ref.shape[0] // n
        for d in range(n):
            held[d * chunk : (d + 1) * chunk, :] = x_ref[rows_of(order_ref, d, chunk), : held.shape[1]]


def project(order_ref, x_ref, wg_ref, wu_ref, far_ref, near_ref, *rest):
    ups, held = rest[:-1], rest[-1]
    chunk = far_ref.shape[1]
    in_order(order_ref, x_ref, held)
    gate = matmul(held[...], wg_ref[...]).astype(BF16)
    up = matmul(held[...], wu_ref[...]).astype(BF16)
    for dx in range(2):
        for dy in range(N_Y):
            at = (dx * N_Y + dy) * chunk
            (near_ref, far_ref)[dx][dy] = gate[at : at + chunk]
            ups[dy][dx] = up[at : at + chunk]


def meet_near(near_ref, got_ref, *outs):
    for dy, out in enumerate(outs, 1):
        out[...] = (near_ref[dy].astype(F32) + got_ref[dy].astype(F32)).astype(BF16)


def meet_far(*refs):
    out = refs[-1]
    out[...] = sum(r[1].astype(F32) for r in refs[:-1]).astype(BF16)


def activate(near_ref, got_ref, g1, g2, g3, u0, u1, u2, u3, got_u, part_ref, *rest):
    outs, (gate_ref, up_ref) = rest[:-2], rest[-2:]
    gate = near_ref[0].astype(F32) + got_ref[0].astype(F32)
    for r in (g1, g2, g3):
        gate = gate + r[...].astype(F32)
    up = got_u[...].astype(F32)
    for r in (u0, u1, u2, u3):
        up = up + r[0].astype(F32)
    gate_ref[...] = gate
    up_ref[...] = up
    hidden = (gate * jax.nn.sigmoid(gate) * up).astype(BF16)
    for d, out in enumerate(outs):
        out[0] = hidden
        out[1] = part_ref[d]


def back(order_ref, c_ref, w_ref, part_ref, load_ref, held):
    slots, cols = held.shape
    chunk = part_ref.shape[1]
    in_order(order_ref, c_ref, held)
    partial = dot(held[...], w_ref[...], ((1,), (1,))).astype(BF16)
    for d in range(part_ref.shape[0]):
        part_ref[d] = partial[d * chunk : (d + 1) * chunk]

    @pl.when(pl.program_id(0) == 0)
    def _():
        counted = ones_where(iota((8, slots), 1) % CAP == iota((8, slots), 0))
        load_ref[...] = matmul(counted, c_ref[:, cols:]).astype(jnp.int32)


def expert(order_ref, w_ref, *rest):
    pieces, (out_ref, hidden_ref) = rest[:-2], rest[-2:]
    chunk = pieces[0].shape[1]
    for d, piece in enumerate(pieces):
        hidden_ref[rows_of(order_ref, d, chunk), :] = piece[0]
    out_ref[...] = matmul(hidden_ref[...], w_ref[...]).astype(BF16)


def back_act(gate_ref, up_ref, *rest):
    parts, (dg_ref, du_ref) = rest[:-2], rest[-2:]
    d = sum(r[1].astype(F32) for r in parts)
    gate = gate_ref[...]
    sigma = jax.nn.sigmoid(gate)
    dg_ref[...] = (d * up_ref[...] * sigma * (1.0 + gate * (1.0 - sigma))).astype(BF16)
    du_ref[...] = (d * gate * sigma).astype(BF16)


def grad_down_tile(hidden_ref, c_ref, out_ref):
    out_ref[...] = matmul(hidden_ref[...].T, c_ref[:, : out_ref.shape[1]]).astype(BF16)


def grad_tile(x_ref, g0, g1, g2, g3, u0, u1, out_g, out_u, held_g, held_u):
    chunk = g0.shape[1]
    for dx in range(2):
        for dy in range(N_Y):
            at = (dx * N_Y + dy) * chunk
            held_g[at : at + chunk, :] = (g0, g1, g2, g3)[dy][dx]
            held_u[at : at + chunk, :] = (u0, u1)[dx][dy]
    x = x_ref[...]
    out_g[...] = matmul(x, held_g[...]).astype(BF16)
    out_u[...] = matmul(x, held_u[...]).astype(BF16)


def combine(hi_ref, lo_ref, y_ref, out_ref):
    y = y_ref[...]
    out = matmul(hi_ref[...], y) * (1.0 / 256.0) + matmul(lo_ref[...], y) * (1.0 / 65536.0)
    out_ref[...] = out.astype(BF16)


def block_at(d):
    me = lax.axis_index("blk")
    return lax.rem(me // N_Y + d // N_Y, 2) * N_Y + lax.rem(me % N_Y + d % N_Y, N_Y)


def move(array, d):
    n = lax.axis_size("blk")
    pairs = [(i, (i // N_Y + d // N_Y) % 2 * N_Y + (i + d) % N_Y) for i in range(n)]
    return lax.ppermute(array, "blk", pairs)


def to_experts(rows, experts):
    cols = rows.shape[-1]
    out = lax.all_to_all(rows.reshape(experts, CAP, cols), "expert", split_axis=0, concat_axis=0, tiled=True)
    return out.reshape(-1, cols)


def body(tokens, cotangent, expert_ids, gate_fixed, w_gate, w_up, w_down):
    experts = lax.axis_size("expert")
    n_blk = lax.axis_size("blk")
    rows, cols = tokens.shape
    ff = w_gate.shape[2]
    slots = experts * CAP
    chunk = slots // n_blk
    steps = ff // TILE
    goes_to = jnp.stack([block_at(d) for d in range(n_blk)])
    comes_from = jnp.stack([block_at((d // N_Y) * N_Y + (-d) % N_Y) for d in range(n_blk)])
    ids = expert_ids.T
    part = (chunk, ff)

    order = (4, 1, 3, 2, 5, 6, 7)

    def tiles(*block):
        zeros = (0,) * (len(block) - 1)
        return pl.BlockSpec(block, lambda i: zeros + (i,))

    def fixed(*block):
        zeros = (0,) * len(block)
        return pl.BlockSpec(block, lambda i: zeros)

    table = pl.BlockSpec(memory_space=pltpu.SMEM)
    (routed_x,) = call(route, [((slots, cols), BF16)], ids, tokens, limit=LARGE)
    arrived = to_experts(routed_x, experts)
    routed_cot, gate_hi, gate_lo = call(
        route_back,
        [((slots, cols + COUNT_LANES), BF16), ((rows, slots), BF16), ((rows, slots), BF16)],
        ids,
        gate_fixed.T,
        cotangent,
        limit=LARGE,
    )
    routed_cot, goes_to, comes_from = lax.optimization_barrier((routed_cot, goes_to, comes_from))
    shapes = [(N_Y, chunk)] * 2 + [(2, chunk)] * N_Y
    far, near, *ups = call(
        project,
        [(a + (ff,), BF16) for a in shapes],
        goes_to,
        arrived,
        w_gate[0],
        w_up[0],
        grid=(steps,),
        in_specs=[table, fixed(slots, cols), tiles(cols, TILE), tiles(cols, TILE)],
        out_specs=[tiles(*a, TILE) for a in shapes],
        scratch_shapes=[pltpu.VMEM((slots, cols), BF16)],
        limit=LARGE,
        flops=4 * slots * cols * ff,
        traffic=7_000_000,
    )
    arrived_cot = to_experts(routed_cot, experts)

    got_far = move(far, N_Y)
    got_ups = [ups[0]] + [move(ups[dy], dy) for dy in range(1, N_Y)]
    (turned,) = call(
        turn,
        [((cols, slots), BF16)],
        comes_from,
        arrived,
        ordered=True,
        scratch_shapes=[pltpu.VMEM((slots, cols), BF16)],
    )
    nears = call(meet_near, [(part, BF16)] * (N_Y - 1), near, got_far)
    (up_far,) = call(meet_far, [(part, BF16)], *got_ups)
    got_nears = [move(g, dy) for dy, g in enumerate(nears, 1)]
    got_up = move(up_far, N_Y)
    got_up, turned = lax.optimization_barrier((got_up, turned))
    parts, loads = call(
        back,
        [((n_blk,) + part, BF16), ((8, COUNT_LANES), jnp.int32)],
        goes_to,
        arrived_cot,
        w_down[0],
        grid=(steps,),
        in_specs=[table, fixed(slots, cols + COUNT_LANES), pl.BlockSpec((TILE, cols), lambda i: (i, 0))],
        out_specs=[tiles(n_blk, chunk, TILE), fixed(8, COUNT_LANES)],
        scratch_shapes=[pltpu.VMEM((slots, cols), BF16)],
        limit=LARGE,
        flops=2 * slots * cols * ff,
        traffic=4_000_000,
    )
    *packs, gate_pre, up_pre = call(
        activate,
        [((2,) + part, BF16)] * n_blk + [(part, F32)] * 2,
        near,
        got_far,
        *got_nears,
        *got_ups,
        got_up,
        parts,
    )
    got = {d: move(packs[d], d) for d in order}
    got = [packs[0]] + [got[d] for d in range(1, n_blk)]
    d_gate, d_up = call(back_act, [(part, BF16)] * 2, gate_pre, up_pre, *got)
    got_dg = move(d_gate, N_Y)
    got_du = [move(d_up, dy) for dy in range(1, N_Y)]
    got, got_dg = lax.optimization_barrier((got, got_dg))
    expert_out, hidden = call(
        expert,
        [((slots, cols), BF16), ((slots, ff), BF16)],
        comes_from,
        w_down[0],
        *got,
        ordered=True,
        limit=LARGE,
        flops=2 * slots * cols * ff,
        traffic=4_000_000,
    )
    returned = to_experts(expert_out, experts)
    dg_pair = jnp.stack([d_gate, got_dg])
    du_four = jnp.stack([d_up] + got_du)
    dg = [dg_pair] + [move(dg_pair, dy) for dy in range(1, N_Y)]
    du = [du_four, move(du_four, N_Y)]
    (grad_down,) = call(
        grad_down_tile,
        [((ff, cols), BF16)],
        hidden,
        arrived_cot,
        grid=(steps,),
        in_specs=[pl.BlockSpec((slots, TILE), lambda i: (0, i)), fixed(slots, cols + COUNT_LANES)],
        out_specs=[pl.BlockSpec((TILE, cols), lambda i: (i, 0))],
        limit=LARGE,
        flops=2 * slots * cols * ff,
        traffic=4_000_000,
    )
    (layer_out,) = call(combine, [((rows, cols), BF16)], gate_hi, gate_lo, returned)
    dg, du, grad_down, layer_out = lax.optimization_barrier((dg, du, grad_down, layer_out))
    grad_gate, grad_up = call(
        grad_tile,
        [((cols, ff), BF16)] * 2,
        turned,
        *dg,
        *du,
        grid=(steps,),
        in_specs=[fixed(cols, slots)] + [tiles(2, chunk, TILE)] * N_Y + [tiles(N_Y, chunk, TILE)] * 2,
        out_specs=[tiles(cols, TILE)] * 2,
        scratch_shapes=[pltpu.VMEM((slots, TILE), BF16)] * 2,
        flops=4 * slots * cols * ff,
        traffic=6_000_000,
    )
    return (layer_out, grad_gate[None], grad_up[None], grad_down[None], loads[:2].reshape(-1))


def solution(mesh):
    return jax.shard_map(
        body,
        mesh=mesh,
        in_specs=(
            P("expert", "blk"),
            P("expert", "blk"),
            P("expert", None),
            P("expert", None),
            P("expert", "blk", None),
            P("expert", "blk", None),
            P("expert", None, "blk"),
        ),
        out_specs=(
            P("expert", "blk"),
            P("expert", "blk", None),
            P("expert", "blk", None),
            P("expert", None, "blk"),
            P(),
        ),
        check_vma=False,
    )
```

```python
import jax
import jax.numpy as jnp
from jax import lax
from jax.experimental import pallas as pl
from jax.experimental.pallas import tpu as pltpu
from jax.sharding import PartitionSpec as P

EXPERTS_ALL = 256
TOPK = 8
CAP = 16
N_Y = 4
TILE = 512
NEAR = 384
F32 = jnp.float32
BF16 = jnp.bfloat16
MIB = 1024 * 1024
SMALL = 16 * MIB
LARGE = 58 * MIB
COUNT_LANES = 128


def iota(shape, dim):
    return lax.broadcasted_iota(jnp.int32, shape, dim)


def dot(left, right, dims):
    return lax.dot_general(left, right, (dims, ((), ())), preferred_element_type=F32)


def matmul(left, right):
    return jnp.dot(left, right, preferred_element_type=F32)


def rows_of(order_ref, d, chunk):
    return pl.ds(pl.multiple_of(order_ref[d] * chunk, chunk), chunk)


def columns_of(i):
    return pl.ds(pl.multiple_of(i * TILE, TILE), TILE)


def whole(array):
    zeros = (0,) * len(array.shape)
    return pl.BlockSpec(array.shape, lambda i: zeros)


def call(kernel, outs, *args, ordered=False, stay=(), limit=SMALL, flops=0, traffic=0, **options):
    outs = [jax.ShapeDtypeStruct(s, t) for s, t in outs]
    in_specs = [whole(a) for a in args]
    if ordered:
        in_specs[0] = pl.BlockSpec(memory_space=pltpu.SMEM)
    for i in stay:
        in_specs[i] = pl.BlockSpec(memory_space=pltpu.HBM)
    settings = dict(grid=(1,), in_specs=in_specs, out_specs=[whole(o) for o in outs])
    settings.update(options)
    return pl.pallas_call(
        kernel,
        out_shape=outs,
        compiler_params=pltpu.CompilerParams(vmem_limit_bytes=limit),
        cost_estimate=pl.CostEstimate(flops=flops, bytes_accessed=traffic, transcendentals=0),
        name=kernel.__name__,
        **settings,
    )(*args)


def ones_where(condition):
    return condition.astype(F32).astype(BF16)


def spread_of(slots, experts):
    return ones_where((iota((slots, experts), 0) // CAP) == iota((slots, experts), 1))


def slots_of(ids_ref, slots):
    rows = ids_ref.shape[1]
    experts = slots // CAP
    line = iota((experts, rows), 0)
    picked = jnp.zeros((experts, rows), F32)
    for k in range(TOPK):
        picked = jnp.where(ids_ref[k : k + 1, :] == line, 1.0, picked)
    rank = matmul(picked.astype(BF16), ones_where(iota((rows, rows), 0) < iota((rows, rows), 1)))
    key = jnp.where(picked > 0.5, rank, -1.0).astype(BF16)
    slot_rank = (iota((slots, rows), 0) % CAP).astype(F32)
    return (matmul(spread_of(slots, experts), key) == slot_rank).astype(F32)


def route(ids_ref, tok_ref, rx_ref):
    sel = slots_of(ids_ref, rx_ref.shape[0]).astype(BF16)
    rx_ref[...] = matmul(sel, tok_ref[...]).astype(BF16)


def route_back(ids_ref, gate_ref, cot_ref, rc_ref, gate_hi_ref, gate_lo_ref):
    rows, cols = cot_ref.shape
    slots = rc_ref.shape[0]
    experts = slots // CAP
    line = iota((experts, rows), 0)
    gate = jnp.zeros((experts, rows), jnp.int32)
    for k in range(TOPK):
        gate = jnp.where(ids_ref[k : k + 1, :] == line, gate_ref[k : k + 1, :], gate)
    spread = spread_of(slots, experts)
    select = slots_of(ids_ref, slots)
    hi = matmul(spread, (gate // 256).astype(F32).astype(BF16)) * select
    lo = matmul(spread, (gate % 256).astype(F32).astype(BF16)) * select
    slot_gate = jnp.sum(hi * 256.0 + lo, axis=1, keepdims=True) * (1.0 / 65536.0)
    rc_ref[:, :cols] = (slot_gate * matmul(select.astype(BF16), cot_ref[...])).astype(BF16)
    gate_hi_ref[...] = hi.T.astype(BF16)
    gate_lo_ref[...] = lo.T.astype(BF16)
    every = iota((EXPERTS_ALL, rows), 0)
    hits = jnp.zeros((EXPERTS_ALL, rows), F32)
    for k in range(TOPK):
        hits = hits + jnp.where(ids_ref[k : k + 1, :] == every, 1.0, 0.0)
    counts = dot(jnp.ones((CAP, rows), BF16), hits.astype(BF16), ((1,), (1,)))
    line = iota((CAP, COUNT_LANES), 0)
    block = jnp.where(line == 0, counts[:, :COUNT_LANES], jnp.where(line == 1, counts[:, COUNT_LANES:], 0.0))
    block = block.astype(BF16)
    for e in range(experts):
        rc_ref[e * CAP : (e + 1) * CAP, cols:] = block


def turn(order_ref, x_ref, out_ref, held):
    chunk = x_ref.shape[0] // order_ref.shape[0]
    for d in range(order_ref.shape[0]):
        held[d * chunk : (d + 1) * chunk, :] = x_ref[rows_of(order_ref, d, chunk), :]
    out_ref[...] = held[...].T


def in_order(order_ref, x_ref, held):
    @pl.when(pl.program_id(0) == 0)
    def _():
        n = order_ref.shape[0]
        chunk = x_ref.shape[0] // n
        for d in range(n):
            held[d * chunk : (d + 1) * chunk, :] = x_ref[rows_of(order_ref, d, chunk), : held.shape[1]]


def project(order_ref, x_ref, wg_ref, wu_ref, far_ref, near_ref, *rest):
    wides, held = rest[:-1], rest[-1]
    chunk = far_ref.shape[1]
    in_order(order_ref, x_ref, held)
    gate = matmul(held[...], wg_ref[...]).astype(BF16)
    up = matmul(held[...], wu_ref[...]).astype(BF16)
    for dx in range(2):
        for dy in range(N_Y):
            at = (dx * N_Y + dy) * chunk
            (near_ref, far_ref)[dx][dy] = gate[at : at + chunk, :NEAR]
            wides[dy][dx, :, : TILE - NEAR] = gate[at : at + chunk, NEAR:]
            wides[dy][dx, :, TILE - NEAR :] = up[at : at + chunk]


def meet_near(near_ref, got_ref, *outs):
    for dy, out in enumerate(outs, 1):
        out[...] = (near_ref[dy].astype(F32) + got_ref[dy].astype(F32)).astype(BF16)


def meet_far(*refs):
    out = refs[-1]
    out[...] = sum(r[1].astype(F32) for r in refs[:-1]).astype(BF16)


def activate(near_ref, got_ref, n1, n2, n3, w0, w1, w2, w3, got_w, part_ref, pack_ref, gate_ref, up_ref):
    near = near_ref[0].astype(F32) + got_ref[0].astype(F32)
    for r in (n1, n2, n3):
        near = near + r[...].astype(F32)
    wide = got_w[...].astype(F32)
    for r in (w0, w1, w2, w3):
        wide = wide + r[0].astype(F32)
    span = 2 * TILE - NEAR
    for i in range(gate_ref.shape[1] // TILE):
        gate_ref[:, i * TILE : i * TILE + NEAR] = near[:, i * NEAR : (i + 1) * NEAR]
        gate_ref[:, i * TILE + NEAR : (i + 1) * TILE] = wide[:, i * span : i * span + TILE - NEAR]
        up_ref[:, i * TILE : (i + 1) * TILE] = wide[:, i * span + TILE - NEAR : (i + 1) * span]
    gate = gate_ref[...]
    hidden = (gate * jax.nn.sigmoid(gate) * up_ref[...]).astype(BF16)
    chunk = hidden.shape[0]
    for d in range(pack_ref.shape[0]):
        pack_ref[d, :chunk] = hidden
        pack_ref[d, chunk:] = part_ref[d]


def back(c_ref, w_ref, part_ref, load_ref):
    slots = c_ref.shape[0]
    cols = w_ref.shape[1]
    chunk = part_ref.shape[1]
    partial = dot(c_ref[:, :cols], w_ref[...], ((1,), (1,))).astype(BF16)
    for d in range(part_ref.shape[0]):
        part_ref[d] = partial[d * chunk : (d + 1) * chunk]

    @pl.when(pl.program_id(0) == 0)
    def _():
        counted = ones_where(iota((8, slots), 1) % CAP == iota((8, slots), 0))
        load_ref[...] = matmul(counted, c_ref[:, cols:]).astype(jnp.int32)


def expert(w_ref, got_ref, out_ref, hidden_ref):
    n, chunk = got_ref.shape[0], got_ref.shape[1]
    for d in range(n):
        hidden_ref[d * chunk : (d + 1) * chunk, :] = got_ref[d]
    out_ref[...] = matmul(hidden_ref[...], w_ref[...]).astype(BF16)


def back_act(gate_ref, up_ref, part_ref, dg_ref, du_ref):
    d = part_ref[0].astype(F32)
    for i in range(1, part_ref.shape[0]):
        d = d + part_ref[i].astype(F32)
    gate = gate_ref[...]
    sigma = jax.nn.sigmoid(gate)
    dg_ref[...] = (d * up_ref[...] * sigma * (1.0 + gate * (1.0 - sigma))).astype(BF16)
    du_ref[...] = (d * gate * sigma).astype(BF16)


def grad_down_tile(hidden_ref, c_ref, out_ref):
    out_ref[...] = matmul(hidden_ref[...].T, c_ref[:, : out_ref.shape[1]]).astype(BF16)


def grad_tile(x_ref, g0, g1, g2, g3, u0, u1, out_g, out_u, held_g, held_u):
    chunk = g0.shape[1]
    for dx in range(2):
        for dy in range(N_Y):
            at = (dx * N_Y + dy) * chunk
            held_g[at : at + chunk, :] = (g0, g1, g2, g3)[dy][dx]
            held_u[at : at + chunk, :] = (u0, u1)[dx][dy]
    x = x_ref[...]
    out_g[...] = matmul(x, held_g[...]).astype(BF16)
    out_u[...] = matmul(x, held_u[...]).astype(BF16)


def combine(hi_ref, lo_ref, y_ref, out_ref):
    y = y_ref[...]
    out = matmul(hi_ref[...], y) * (1.0 / 256.0) + matmul(lo_ref[...], y) * (1.0 / 65536.0)
    out_ref[...] = out.astype(BF16)


def block_at(d):
    me = lax.axis_index("blk")
    return lax.rem(me // N_Y + d // N_Y, 2) * N_Y + lax.rem(me % N_Y + d % N_Y, N_Y)


def move(array, d):
    n = lax.axis_size("blk")
    pairs = [(i, (i // N_Y + d // N_Y) % 2 * N_Y + (i + d) % N_Y) for i in range(n)]
    return lax.ppermute(array, "blk", pairs)


def to_experts(rows, experts):
    cols = rows.shape[-1]
    out = lax.all_to_all(rows.reshape(experts, CAP, cols), "expert", split_axis=0, concat_axis=0, tiled=True)
    return out.reshape(-1, cols)


def body(tokens, cotangent, expert_ids, gate_fixed, w_gate, w_up, w_down):
    experts = lax.axis_size("expert")
    n_blk = lax.axis_size("blk")
    rows, cols = tokens.shape
    ff = w_gate.shape[2]
    slots = experts * CAP
    chunk = slots // n_blk
    steps = ff // TILE
    goes_to = jnp.stack([block_at(d) for d in range(n_blk)])
    comes_from = jnp.stack([block_at((d // N_Y) * N_Y + (-d) % N_Y) for d in range(n_blk)])
    ids = expert_ids.T
    part = (chunk, ff)

    order = (3, 4, 1, 2, 5, 6, 7)

    def tiles(*block):
        zeros = (0,) * (len(block) - 1)
        return pl.BlockSpec(block, lambda i: zeros + (i,))

    def fixed(*block):
        zeros = (0,) * len(block)
        return pl.BlockSpec(block, lambda i: zeros)

    table = pl.BlockSpec(memory_space=pltpu.SMEM)
    (routed_x,) = call(route, [((slots, cols), BF16)], ids, tokens, limit=LARGE)
    arrived = to_experts(routed_x, experts)
    routed_cot, gate_hi, gate_lo = call(
        route_back,
        [((slots, cols + COUNT_LANES), BF16), ((rows, slots), BF16), ((rows, slots), BF16)],
        ids,
        gate_fixed.T,
        cotangent,
        limit=LARGE,
    )
    routed_cot, goes_to, comes_from = lax.optimization_barrier((routed_cot, goes_to, comes_from))
    span = 2 * TILE - NEAR
    shapes = [(N_Y, chunk, NEAR)] * 2 + [(2, chunk, span)] * N_Y
    far, near, *ups = call(
        project,
        [(a[:2] + (a[2] * steps,), BF16) for a in shapes],
        goes_to,
        arrived,
        w_gate[0],
        w_up[0],
        grid=(steps,),
        in_specs=[table, fixed(slots, cols), tiles(cols, TILE), tiles(cols, TILE)],
        out_specs=[tiles(*a) for a in shapes],
        scratch_shapes=[pltpu.VMEM((slots, cols), BF16)],
        limit=LARGE,
        flops=4 * slots * cols * ff,
        traffic=7_000_000,
    )
    arrived_cot = to_experts(routed_cot, experts)

    got_far = move(far, N_Y)
    got_ups = [ups[0]] + [move(ups[dy], dy) for dy in range(1, N_Y)]
    (turned,) = call(
        turn,
        [((cols, slots), BF16)],
        comes_from,
        arrived,
        ordered=True,
        scratch_shapes=[pltpu.VMEM((slots, cols), BF16)],
    )
    nears = call(meet_near, [((chunk, NEAR * steps), BF16)] * (N_Y - 1), near, got_far)
    (up_far,) = call(meet_far, [((chunk, span * steps), BF16)], *got_ups)
    got_nears = [move(g, dy) for dy, g in enumerate(nears, 1)]
    got_up = move(up_far, N_Y)
    parts, loads = call(
        back,
        [((n_blk,) + part, BF16), ((8, COUNT_LANES), jnp.int32)],
        arrived_cot,
        w_down[0],
        grid=(steps,),
        in_specs=[fixed(slots, cols + COUNT_LANES), pl.BlockSpec((TILE, cols), lambda i: (i, 0))],
        out_specs=[tiles(n_blk, chunk, TILE), fixed(8, COUNT_LANES)],
        limit=LARGE,
        flops=2 * slots * cols * ff,
        traffic=4_000_000,
    )
    pack, gate_pre, up_pre = call(
        activate,
        [((n_blk, 2 * chunk, ff), BF16), (part, F32), (part, F32)],
        near,
        got_far,
        *got_nears,
        *got_ups,
        got_up,
        parts,
    )
    got = lax.all_to_all(pack, "blk", split_axis=0, concat_axis=0, tiled=True)
    (d_gate, d_up) = call(
        back_act,
        [(part, BF16)] * 2,
        gate_pre,
        up_pre,
        got,
        in_specs=[fixed(*part), fixed(*part), pl.BlockSpec((n_blk, chunk, ff), lambda i: (0, 1, 0))],
    )
    got_dg = move(d_gate, N_Y)
    got_du = [move(d_up, dy) for dy in range(1, N_Y)]
    expert_out, hidden = call(
        expert,
        [((slots, cols), BF16), ((slots, ff), BF16)],
        w_down[0],
        got,
        in_specs=[fixed(ff, cols), fixed(n_blk, chunk, ff)],
        limit=LARGE,
        flops=2 * slots * cols * ff,
        traffic=4_000_000,
    )
    returned = to_experts(expert_out, experts)
    dg_pair = jnp.stack([d_gate, got_dg])
    du_four = jnp.stack([d_up] + got_du)
    dg = [dg_pair] + [move(dg_pair, dy) for dy in range(1, N_Y)]
    du = [du_four, move(du_four, N_Y)]
    (grad_down,) = call(
        grad_down_tile,
        [((ff, cols), BF16)],
        hidden,
        arrived_cot,
        grid=(steps,),
        in_specs=[pl.BlockSpec((slots, TILE), lambda i: (0, i)), fixed(slots, cols + COUNT_LANES)],
        out_specs=[pl.BlockSpec((TILE, cols), lambda i: (i, 0))],
        limit=LARGE,
        flops=2 * slots * cols * ff,
        traffic=4_000_000,
    )
    (layer_out,) = call(combine, [((rows, cols), BF16)], gate_hi, gate_lo, returned)
    dg, du, grad_down, layer_out, turned = lax.optimization_barrier((dg, du, grad_down, layer_out, turned))
    grad_gate, grad_up = call(
        grad_tile,
        [((cols, ff), BF16)] * 2,
        turned,
        *dg,
        *du,
        grid=(steps,),
        in_specs=[fixed(cols, slots)] + [tiles(2, chunk, TILE)] * N_Y + [tiles(N_Y, chunk, TILE)] * 2,
        out_specs=[tiles(cols, TILE)] * 2,
        scratch_shapes=[pltpu.VMEM((slots, TILE), BF16)] * 2,
        flops=4 * slots * cols * ff,
        traffic=6_000_000,
    )
    return (layer_out, grad_gate[None], grad_up[None], grad_down[None], loads[:2].reshape(-1))


def solution(mesh):
    return jax.shard_map(
        body,
        mesh=mesh,
        in_specs=(
            P("expert", "blk"),
            P("expert", "blk"),
            P("expert", None),
            P("expert", None),
            P("expert", "blk", None),
            P("expert", "blk", None),
            P("expert", None, "blk"),
        ),
        out_specs=(
            P("expert", "blk"),
            P("expert", "blk", None),
            P("expert", "blk", None),
            P("expert", None, "blk"),
            P(),
        ),
        check_vma=False,
    )
```

```python
import jax
import jax.numpy as jnp
from jax import lax
from jax.experimental import pallas as pl
from jax.experimental.pallas import tpu as pltpu
from jax.sharding import PartitionSpec as P

EXPERTS_ALL = 256
TOPK = 8
CAP = 16
N_Y = 4
TILE = 512
NEAR = 384
F32 = jnp.float32
BF16 = jnp.bfloat16
MIB = 1024 * 1024
SMALL = 16 * MIB
LARGE = 58 * MIB
COUNT_LANES = 128


def iota(shape, dim):
    return lax.broadcasted_iota(jnp.int32, shape, dim)


def dot(left, right, dims):
    return lax.dot_general(left, right, (dims, ((), ())), preferred_element_type=F32)


def matmul(left, right):
    return jnp.dot(left, right, preferred_element_type=F32)


def rows_of(order_ref, d, chunk):
    return pl.ds(pl.multiple_of(order_ref[d] * chunk, chunk), chunk)


def columns_of(i):
    return pl.ds(pl.multiple_of(i * TILE, TILE), TILE)


def whole(array):
    zeros = (0,) * len(array.shape)
    return pl.BlockSpec(array.shape, lambda i: zeros)


def call(kernel, outs, *args, ordered=False, stay=(), limit=SMALL, flops=0, traffic=0, **options):
    outs = [jax.ShapeDtypeStruct(s, t) for s, t in outs]
    in_specs = [whole(a) for a in args]
    if ordered:
        in_specs[0] = pl.BlockSpec(memory_space=pltpu.SMEM)
    for i in stay:
        in_specs[i] = pl.BlockSpec(memory_space=pltpu.HBM)
    settings = dict(grid=(1,), in_specs=in_specs, out_specs=[whole(o) for o in outs])
    settings.update(options)
    return pl.pallas_call(
        kernel,
        out_shape=outs,
        compiler_params=pltpu.CompilerParams(vmem_limit_bytes=limit),
        cost_estimate=pl.CostEstimate(flops=flops, bytes_accessed=traffic, transcendentals=0),
        name=kernel.__name__,
        **settings,
    )(*args)


def ones_where(condition):
    return condition.astype(F32).astype(BF16)


def spread_of(slots, experts):
    return ones_where((iota((slots, experts), 0) // CAP) == iota((slots, experts), 1))


def slots_of(ids_ref, slots):
    rows = ids_ref.shape[1]
    experts = slots // CAP
    line = iota((experts, rows), 0)
    picked = jnp.zeros((experts, rows), F32)
    for k in range(TOPK):
        picked = jnp.where(ids_ref[k : k + 1, :] == line, 1.0, picked)
    rank = matmul(picked.astype(BF16), ones_where(iota((rows, rows), 0) < iota((rows, rows), 1)))
    key = jnp.where(picked > 0.5, rank, -1.0).astype(BF16)
    slot_rank = (iota((slots, rows), 0) % CAP).astype(F32)
    return (matmul(spread_of(slots, experts), key) == slot_rank).astype(F32)


def route(ids_ref, tok_ref, rx_ref):
    sel = slots_of(ids_ref, rx_ref.shape[0]).astype(BF16)
    rx_ref[...] = matmul(sel, tok_ref[...]).astype(BF16)


def route_back(ids_ref, gate_ref, cot_ref, rc_ref, gate_hi_ref, gate_lo_ref):
    rows, cols = cot_ref.shape
    slots = rc_ref.shape[0]
    experts = slots // CAP
    line = iota((experts, rows), 0)
    gate = jnp.zeros((experts, rows), jnp.int32)
    for k in range(TOPK):
        gate = jnp.where(ids_ref[k : k + 1, :] == line, gate_ref[k : k + 1, :], gate)
    spread = spread_of(slots, experts)
    select = slots_of(ids_ref, slots)
    hi = matmul(spread, (gate // 256).astype(F32).astype(BF16)) * select
    lo = matmul(spread, (gate % 256).astype(F32).astype(BF16)) * select
    slot_gate = jnp.sum(hi * 256.0 + lo, axis=1, keepdims=True) * (1.0 / 65536.0)
    rc_ref[:, :cols] = (slot_gate * matmul(select.astype(BF16), cot_ref[...])).astype(BF16)
    gate_hi_ref[...] = hi.T.astype(BF16)
    gate_lo_ref[...] = lo.T.astype(BF16)
    every = iota((EXPERTS_ALL, rows), 0)
    hits = jnp.zeros((EXPERTS_ALL, rows), F32)
    for k in range(TOPK):
        hits = hits + jnp.where(ids_ref[k : k + 1, :] == every, 1.0, 0.0)
    counts = dot(jnp.ones((CAP, rows), BF16), hits.astype(BF16), ((1,), (1,)))
    line = iota((CAP, COUNT_LANES), 0)
    block = jnp.where(line == 0, counts[:, :COUNT_LANES], jnp.where(line == 1, counts[:, COUNT_LANES:], 0.0))
    block = block.astype(BF16)
    for e in range(experts):
        rc_ref[e * CAP : (e + 1) * CAP, cols:] = block


def turn(order_ref, x_ref, out_ref, held):
    chunk = x_ref.shape[0] // order_ref.shape[0]
    for d in range(order_ref.shape[0]):
        held[d * chunk : (d + 1) * chunk, :] = x_ref[rows_of(order_ref, d, chunk), :]
    out_ref[...] = held[...].T


def in_order(order_ref, x_ref, held):
    @pl.when(pl.program_id(0) == 0)
    def _():
        n = order_ref.shape[0]
        chunk = x_ref.shape[0] // n
        for d in range(n):
            held[d * chunk : (d + 1) * chunk, :] = x_ref[rows_of(order_ref, d, chunk), : held.shape[1]]


def project(order_ref, x_ref, wg_ref, wu_ref, far_ref, near_ref, *rest):
    wides, held = rest[:-1], rest[-1]
    chunk = far_ref.shape[1]
    in_order(order_ref, x_ref, held)
    gate = matmul(held[...], wg_ref[...]).astype(BF16)
    up = matmul(held[...], wu_ref[...]).astype(BF16)
    for dx in range(2):
        for dy in range(N_Y):
            at = (dx * N_Y + dy) * chunk
            (near_ref, far_ref)[dx][dy] = gate[at : at + chunk, :NEAR]
            wides[dy][dx, :, : TILE - NEAR] = gate[at : at + chunk, NEAR:]
            wides[dy][dx, :, TILE - NEAR :] = up[at : at + chunk]


def meet_near(near_ref, got_ref, *outs):
    for dy, out in enumerate(outs, 1):
        out[...] = (near_ref[dy].astype(F32) + got_ref[dy].astype(F32)).astype(BF16)


def meet_far(*refs):
    out = refs[-1]
    out[...] = sum(r[1].astype(F32) for r in refs[:-1]).astype(BF16)


def activate(near_ref, got_ref, n1, n2, n3, w0, w1, w2, w3, got_w, pack_ref, gate_ref, up_ref):
    near = near_ref[0].astype(F32) + got_ref[0].astype(F32)
    for r in (n1, n2, n3):
        near = near + r[...].astype(F32)
    wide = got_w[...].astype(F32)
    for r in (w0, w1, w2, w3):
        wide = wide + r[0].astype(F32)
    span = 2 * TILE - NEAR
    for i in range(gate_ref.shape[1] // TILE):
        gate_ref[:, i * TILE : i * TILE + NEAR] = near[:, i * NEAR : (i + 1) * NEAR]
        gate_ref[:, i * TILE + NEAR : (i + 1) * TILE] = wide[:, i * span : i * span + TILE - NEAR]
        up_ref[:, i * TILE : (i + 1) * TILE] = wide[:, i * span + TILE - NEAR : (i + 1) * span]
    gate = gate_ref[...]
    hidden = (gate * jax.nn.sigmoid(gate) * up_ref[...]).astype(BF16)
    for d in range(pack_ref.shape[0]):
        pack_ref[d] = hidden


def back(order_ref, c_ref, w_ref, *rest):
    outs, (load_ref, held) = rest[:-2], rest[-2:]
    slots, cols = held.shape
    chunk = outs[0].shape[1]
    in_order(order_ref, c_ref, held)
    partial = dot(held[...], w_ref[...], ((1,), (1,))).astype(BF16)
    for dx in range(2):
        for dy, out in enumerate(outs):
            at = (dx * N_Y + dy) * chunk
            out[dx] = partial[at : at + chunk]

    @pl.when(pl.program_id(0) == 0)
    def _():
        counted = ones_where(iota((8, slots), 1) % CAP == iota((8, slots), 0))
        load_ref[...] = matmul(counted, c_ref[:, cols:]).astype(jnp.int32)


def expert(w_ref, hidden_ref, out_ref):
    out_ref[...] = matmul(hidden_ref[...], w_ref[...]).astype(BF16)


def back_act(gate_ref, up_ref, p0, p1, p2, p3, got, dg_ref, du_ref):
    d = got[...].astype(F32)
    for r in (p0, p1, p2, p3):
        d = d + r[0].astype(F32)
    gate = gate_ref[...]
    sigma = jax.nn.sigmoid(gate)
    dg_ref[...] = (d * up_ref[...] * sigma * (1.0 + gate * (1.0 - sigma))).astype(BF16)
    du_ref[...] = (d * gate * sigma).astype(BF16)


def grad_down_tile(hidden_ref, c_ref, out_ref):
    out_ref[...] = matmul(hidden_ref[...].T, c_ref[:, : out_ref.shape[1]]).astype(BF16)


def grad_tile(x_ref, g0, g1, g2, g3, u0, u1, out_g, out_u, held_g, held_u):
    chunk = g0.shape[1]
    for dx in range(2):
        for dy in range(N_Y):
            at = (dx * N_Y + dy) * chunk
            held_g[at : at + chunk, :] = (g0, g1, g2, g3)[dy][dx]
            held_u[at : at + chunk, :] = (u0, u1)[dx][dy]
    x = x_ref[...]
    out_g[...] = matmul(x, held_g[...]).astype(BF16)
    out_u[...] = matmul(x, held_u[...]).astype(BF16)


def combine(hi_ref, lo_ref, y_ref, out_ref):
    y = y_ref[...]
    out = matmul(hi_ref[...], y) * (1.0 / 256.0) + matmul(lo_ref[...], y) * (1.0 / 65536.0)
    out_ref[...] = out.astype(BF16)


def block_at(d):
    me = lax.axis_index("blk")
    return lax.rem(me // N_Y + d // N_Y, 2) * N_Y + lax.rem(me % N_Y + d % N_Y, N_Y)


def move(array, d):
    n = lax.axis_size("blk")
    pairs = [(i, (i // N_Y + d // N_Y) % 2 * N_Y + (i + d) % N_Y) for i in range(n)]
    return lax.ppermute(array, "blk", pairs)


def to_experts(rows, experts):
    cols = rows.shape[-1]
    out = lax.all_to_all(rows.reshape(experts, CAP, cols), "expert", split_axis=0, concat_axis=0, tiled=True)
    return out.reshape(-1, cols)


def body(tokens, cotangent, expert_ids, gate_fixed, w_gate, w_up, w_down):
    experts = lax.axis_size("expert")
    n_blk = lax.axis_size("blk")
    rows, cols = tokens.shape
    ff = w_gate.shape[2]
    slots = experts * CAP
    chunk = slots // n_blk
    steps = ff // TILE
    goes_to = jnp.stack([block_at(d) for d in range(n_blk)])
    comes_from = jnp.stack([block_at((d // N_Y) * N_Y + (-d) % N_Y) for d in range(n_blk)])
    ids = expert_ids.T
    part = (chunk, ff)

    order = (3, 4, 1, 2, 5, 6, 7)

    def tiles(*block):
        zeros = (0,) * (len(block) - 1)
        return pl.BlockSpec(block, lambda i: zeros + (i,))

    def fixed(*block):
        zeros = (0,) * len(block)
        return pl.BlockSpec(block, lambda i: zeros)

    table = pl.BlockSpec(memory_space=pltpu.SMEM)
    (routed_x,) = call(route, [((slots, cols), BF16)], ids, tokens, limit=LARGE)
    arrived = to_experts(routed_x, experts)
    routed_cot, gate_hi, gate_lo = call(
        route_back,
        [((slots, cols + COUNT_LANES), BF16), ((rows, slots), BF16), ((rows, slots), BF16)],
        ids,
        gate_fixed.T,
        cotangent,
        limit=LARGE,
    )
    routed_cot, goes_to, comes_from = lax.optimization_barrier((routed_cot, goes_to, comes_from))
    span = 2 * TILE - NEAR
    shapes = [(N_Y, chunk, NEAR)] * 2 + [(2, chunk, span)] * N_Y
    far, near, *ups = call(
        project,
        [(a[:2] + (a[2] * steps,), BF16) for a in shapes],
        goes_to,
        arrived,
        w_gate[0],
        w_up[0],
        grid=(steps,),
        in_specs=[table, fixed(slots, cols), tiles(cols, TILE), tiles(cols, TILE)],
        out_specs=[tiles(*a) for a in shapes],
        scratch_shapes=[pltpu.VMEM((slots, cols), BF16)],
        limit=LARGE,
        flops=4 * slots * cols * ff,
        traffic=7_000_000,
    )
    arrived_cot = to_experts(routed_cot, experts)

    got_far = move(far, N_Y)
    got_ups = [ups[0]] + [move(ups[dy], dy) for dy in range(1, N_Y)]
    nears = call(meet_near, [((chunk, NEAR * steps), BF16)] * (N_Y - 1), near, got_far)
    (up_far,) = call(meet_far, [((chunk, span * steps), BF16)], *got_ups)
    got_nears = [move(g, dy) for dy, g in enumerate(nears, 1)]
    got_up = move(up_far, N_Y)
    *parts, loads = call(
        back,
        [((2,) + part, BF16)] * N_Y + [((8, COUNT_LANES), jnp.int32)],
        goes_to,
        arrived_cot,
        w_down[0],
        grid=(steps,),
        in_specs=[table, fixed(slots, cols + COUNT_LANES), pl.BlockSpec((TILE, cols), lambda i: (i, 0))],
        out_specs=[tiles(2, chunk, TILE)] * N_Y + [fixed(8, COUNT_LANES)],
        scratch_shapes=[pltpu.VMEM((slots, cols), BF16)],
        limit=LARGE,
        flops=2 * slots * cols * ff,
        traffic=4_000_000,
    )
    hidden, gate_pre, up_pre = call(
        activate,
        [((n_blk,) + part, BF16), (part, F32), (part, F32)],
        near,
        got_far,
        *got_nears,
        *got_ups,
        got_up,
    )
    hidden = lax.all_to_all(hidden, "blk", split_axis=0, concat_axis=0, tiled=True).reshape(slots, ff)
    got = [parts[0]] + [move(parts[dy], dy) for dy in range(1, N_Y)]
    (expert_out,) = call(
        expert,
        [((slots, cols), BF16)],
        w_down[0],
        hidden,
        limit=LARGE,
        flops=2 * slots * cols * ff,
        traffic=4_000_000,
    )
    returned = to_experts(expert_out, experts)
    (d_far,) = call(meet_far, [(part, BF16)], *got, flops=10**11)
    got_d = move(d_far, N_Y)
    d_gate, d_up = call(back_act, [(part, BF16)] * 2, gate_pre, up_pre, *got, got_d)
    got_dg = move(d_gate, N_Y)
    got_du = [move(d_up, dy) for dy in range(1, N_Y)]
    dg_pair = jnp.stack([d_gate, got_dg])
    du_four = jnp.stack([d_up] + got_du)
    dg = [dg_pair] + [move(dg_pair, dy) for dy in range(1, N_Y)]
    du = [du_four, move(du_four, N_Y)]
    (grad_down,) = call(
        grad_down_tile,
        [((ff, cols), BF16)],
        hidden,
        arrived_cot,
        grid=(steps,),
        in_specs=[pl.BlockSpec((slots, TILE), lambda i: (0, i)), fixed(slots, cols + COUNT_LANES)],
        out_specs=[pl.BlockSpec((TILE, cols), lambda i: (i, 0))],
        limit=LARGE,
        flops=2 * slots * cols * ff,
        traffic=4_000_000,
    )
    arrived, grad_down = lax.optimization_barrier((arrived, grad_down))
    (turned,) = call(
        turn,
        [((cols, slots), BF16)],
        comes_from,
        arrived,
        ordered=True,
        scratch_shapes=[pltpu.VMEM((slots, cols), BF16)],
    )
    (layer_out,) = call(combine, [((rows, cols), BF16)], gate_hi, gate_lo, returned)
    dg, du, grad_down, layer_out, turned = lax.optimization_barrier((dg, du, grad_down, layer_out, turned))
    grad_gate, grad_up = call(
        grad_tile,
        [((cols, ff), BF16)] * 2,
        turned,
        *dg,
        *du,
        grid=(steps,),
        in_specs=[fixed(cols, slots)] + [tiles(2, chunk, TILE)] * N_Y + [tiles(N_Y, chunk, TILE)] * 2,
        out_specs=[tiles(cols, TILE)] * 2,
        scratch_shapes=[pltpu.VMEM((slots, TILE), BF16)] * 2,
        flops=4 * slots * cols * ff,
        traffic=6_000_000,
    )
    return (layer_out, grad_gate[None], grad_up[None], grad_down[None], loads[:2].reshape(-1))


def solution(mesh):
    return jax.shard_map(
        body,
        mesh=mesh,
        in_specs=(
            P("expert", "blk"),
            P("expert", "blk"),
            P("expert", None),
            P("expert", None),
            P("expert", "blk", None),
            P("expert", "blk", None),
            P("expert", None, "blk"),
        ),
        out_specs=(
            P("expert", "blk"),
            P("expert", "blk", None),
            P("expert", "blk", None),
            P("expert", None, "blk"),
            P(),
        ),
        check_vma=False,
    )
```

```python
import jax
import jax.numpy as jnp
from jax import lax
from jax.experimental import pallas as pl
from jax.experimental.pallas import tpu as pltpu
from jax.sharding import PartitionSpec as P

EXPERTS_ALL = 256
TOPK = 8
CAP = 16
N_Y = 4
TILE = 512
NEAR = 384
F32 = jnp.float32
BF16 = jnp.bfloat16
MIB = 1024 * 1024
SMALL = 16 * MIB
LARGE = 58 * MIB
COUNT_LANES = 128


def iota(shape, dim):
    return lax.broadcasted_iota(jnp.int32, shape, dim)


def dot(left, right, dims):
    return lax.dot_general(left, right, (dims, ((), ())), preferred_element_type=F32)


def matmul(left, right):
    return jnp.dot(left, right, preferred_element_type=F32)


def rows_of(order_ref, d, chunk):
    return pl.ds(pl.multiple_of(order_ref[d] * chunk, chunk), chunk)


def columns_of(i):
    return pl.ds(pl.multiple_of(i * TILE, TILE), TILE)


def whole(array):
    zeros = (0,) * len(array.shape)
    return pl.BlockSpec(array.shape, lambda i: zeros)


def call(kernel, outs, *args, ordered=False, stay=(), limit=SMALL, flops=0, traffic=0, **options):
    outs = [jax.ShapeDtypeStruct(s, t) for s, t in outs]
    in_specs = [whole(a) for a in args]
    if ordered:
        in_specs[0] = pl.BlockSpec(memory_space=pltpu.SMEM)
    for i in stay:
        in_specs[i] = pl.BlockSpec(memory_space=pltpu.HBM)
    settings = dict(grid=(1,), in_specs=in_specs, out_specs=[whole(o) for o in outs])
    settings.update(options)
    return pl.pallas_call(
        kernel,
        out_shape=outs,
        compiler_params=pltpu.CompilerParams(vmem_limit_bytes=limit),
        cost_estimate=pl.CostEstimate(flops=flops, bytes_accessed=traffic, transcendentals=0),
        name=kernel.__name__,
        **settings,
    )(*args)


def ones_where(condition):
    return condition.astype(F32).astype(BF16)


def spread_of(slots, experts):
    return ones_where((iota((slots, experts), 0) // CAP) == iota((slots, experts), 1))


def slots_of(ids_ref, slots):
    rows = ids_ref.shape[1]
    experts = slots // CAP
    line = iota((experts, rows), 0)
    picked = jnp.zeros((experts, rows), F32)
    for k in range(TOPK):
        picked = jnp.where(ids_ref[k : k + 1, :] == line, 1.0, picked)
    rank = matmul(picked.astype(BF16), ones_where(iota((rows, rows), 0) < iota((rows, rows), 1)))
    key = jnp.where(picked > 0.5, rank, -1.0).astype(BF16)
    slot_rank = (iota((slots, rows), 0) % CAP).astype(F32)
    return (matmul(spread_of(slots, experts), key) == slot_rank).astype(F32)


def route(ids_ref, tok_ref, rx_ref):
    sel = slots_of(ids_ref, rx_ref.shape[0]).astype(BF16)
    rx_ref[...] = matmul(sel, tok_ref[...]).astype(BF16)


def route_back(ids_ref, gate_ref, cot_ref, rc_ref, gate_hi_ref, gate_lo_ref):
    rows, cols = cot_ref.shape
    slots = rc_ref.shape[0]
    experts = slots // CAP
    line = iota((experts, rows), 0)
    gate = jnp.zeros((experts, rows), jnp.int32)
    for k in range(TOPK):
        gate = jnp.where(ids_ref[k : k + 1, :] == line, gate_ref[k : k + 1, :], gate)
    spread = spread_of(slots, experts)
    select = slots_of(ids_ref, slots)
    hi = matmul(spread, (gate // 256).astype(F32).astype(BF16)) * select
    lo = matmul(spread, (gate % 256).astype(F32).astype(BF16)) * select
    slot_gate = jnp.sum(hi * 256.0 + lo, axis=1, keepdims=True) * (1.0 / 65536.0)
    rc_ref[:, :cols] = (slot_gate * matmul(select.astype(BF16), cot_ref[...])).astype(BF16)
    gate_hi_ref[...] = hi.T.astype(BF16)
    gate_lo_ref[...] = lo.T.astype(BF16)
    every = iota((EXPERTS_ALL, rows), 0)
    hits = jnp.zeros((EXPERTS_ALL, rows), F32)
    for k in range(TOPK):
        hits = hits + jnp.where(ids_ref[k : k + 1, :] == every, 1.0, 0.0)
    counts = dot(jnp.ones((CAP, rows), BF16), hits.astype(BF16), ((1,), (1,)))
    line = iota((CAP, COUNT_LANES), 0)
    block = jnp.where(line == 0, counts[:, :COUNT_LANES], jnp.where(line == 1, counts[:, COUNT_LANES:], 0.0))
    block = block.astype(BF16)
    for e in range(experts):
        rc_ref[e * CAP : (e + 1) * CAP, cols:] = block


def turn(order_ref, x_ref, out_ref, held):
    chunk = x_ref.shape[0] // order_ref.shape[0]
    for d in range(order_ref.shape[0]):
        held[d * chunk : (d + 1) * chunk, :] = x_ref[rows_of(order_ref, d, chunk), :]
    out_ref[...] = held[...].T


def in_order(order_ref, x_ref, held):
    @pl.when(pl.program_id(0) == 0)
    def _():
        n = order_ref.shape[0]
        chunk = x_ref.shape[0] // n
        for d in range(n):
            held[d * chunk : (d + 1) * chunk, :] = x_ref[rows_of(order_ref, d, chunk), : held.shape[1]]


def project(order_ref, x_ref, wg_ref, wu_ref, far_ref, near_ref, *rest):
    wides, held = rest[:-1], rest[-1]
    chunk = far_ref.shape[1]
    in_order(order_ref, x_ref, held)
    gate = matmul(held[...], wg_ref[...]).astype(BF16)
    up = matmul(held[...], wu_ref[...]).astype(BF16)
    for dx in range(2):
        for dy in range(N_Y):
            at = (dx * N_Y + dy) * chunk
            (near_ref, far_ref)[dx][dy] = gate[at : at + chunk, :NEAR]
            wides[dy][dx, :, : TILE - NEAR] = gate[at : at + chunk, NEAR:]
            wides[dy][dx, :, TILE - NEAR :] = up[at : at + chunk]


def meet_near(near_ref, got_ref, *outs):
    for dy, out in enumerate(outs, 1):
        out[...] = (near_ref[dy].astype(F32) + got_ref[dy].astype(F32)).astype(BF16)


def meet_far(*refs):
    out = refs[-1]
    out[...] = sum(r[1].astype(F32) for r in refs[:-1]).astype(BF16)


def activate(near_ref, got_ref, n1, n2, n3, w0, w1, w2, w3, got_w, pack_ref, gate_ref, up_ref):
    near = near_ref[0].astype(F32) + got_ref[0].astype(F32)
    for r in (n1, n2, n3):
        near = near + r[...].astype(F32)
    wide = got_w[...].astype(F32)
    for r in (w0, w1, w2, w3):
        wide = wide + r[0].astype(F32)
    span = 2 * TILE - NEAR
    for i in range(gate_ref.shape[1] // TILE):
        gate_ref[:, i * TILE : i * TILE + NEAR] = near[:, i * NEAR : (i + 1) * NEAR]
        gate_ref[:, i * TILE + NEAR : (i + 1) * TILE] = wide[:, i * span : i * span + TILE - NEAR]
        up_ref[:, i * TILE : (i + 1) * TILE] = wide[:, i * span + TILE - NEAR : (i + 1) * span]
    gate = gate_ref[...]
    hidden = (gate * jax.nn.sigmoid(gate) * up_ref[...]).astype(BF16)
    for d in range(pack_ref.shape[0]):
        pack_ref[d] = hidden


def back(order_ref, c_ref, w_ref, *rest):
    outs, (load_ref, held) = rest[:-2], rest[-2:]
    slots, cols = held.shape
    chunk = outs[0].shape[1]
    in_order(order_ref, c_ref, held)
    partial = dot(held[...], w_ref[...], ((1,), (1,))).astype(BF16)
    for dx in range(2):
        for dy, out in enumerate(outs):
            at = (dx * N_Y + dy) * chunk
            out[dx] = partial[at : at + chunk]

    @pl.when(pl.program_id(0) == 0)
    def _():
        counted = ones_where(iota((8, slots), 1) % CAP == iota((8, slots), 0))
        load_ref[...] = matmul(counted, c_ref[:, cols:]).astype(jnp.int32)


def expert(w_ref, hidden_ref, out_ref):
    out_ref[...] = matmul(hidden_ref[...], w_ref[...]).astype(BF16)


def back_act(gate_ref, up_ref, p0, p1, p2, p3, got, dg_ref, du_ref):
    d = got[...].astype(F32)
    for r in (p0, p1, p2, p3):
        d = d + r[0].astype(F32)
    gate = gate_ref[...]
    sigma = jax.nn.sigmoid(gate)
    dg_ref[...] = (d * up_ref[...] * sigma * (1.0 + gate * (1.0 - sigma))).astype(BF16)
    du_ref[...] = (d * gate * sigma).astype(BF16)


def grad_down_tile(hidden_ref, c_ref, out_ref):
    out_ref[...] = matmul(hidden_ref[...].T, c_ref[:, : out_ref.shape[1]]).astype(BF16)


def grad_tile(x_ref, g0, g1, g2, g3, u0, u1, out_g, out_u, held_g, held_u):
    chunk = g0.shape[1]
    for dx in range(2):
        for dy in range(N_Y):
            at = (dx * N_Y + dy) * chunk
            held_g[at : at + chunk, :] = (g0, g1, g2, g3)[dy][dx]
            held_u[at : at + chunk, :] = (u0, u1)[dx][dy]
    x = x_ref[...]
    out_g[...] = matmul(x, held_g[...]).astype(BF16)
    out_u[...] = matmul(x, held_u[...]).astype(BF16)


def combine(hi_ref, lo_ref, y_ref, out_ref):
    y = y_ref[...]
    out = matmul(hi_ref[...], y) * (1.0 / 256.0) + matmul(lo_ref[...], y) * (1.0 / 65536.0)
    out_ref[...] = out.astype(BF16)


def block_at(d):
    me = lax.axis_index("blk")
    return lax.rem(me // N_Y + d // N_Y, 2) * N_Y + lax.rem(me % N_Y + d % N_Y, N_Y)


def move(array, d):
    n = lax.axis_size("blk")
    pairs = [(i, (i // N_Y + d // N_Y) % 2 * N_Y + (i + d) % N_Y) for i in range(n)]
    return lax.ppermute(array, "blk", pairs)


def to_experts(rows, experts):
    cols = rows.shape[-1]
    out = lax.all_to_all(rows.reshape(experts, CAP, cols), "expert", split_axis=0, concat_axis=0, tiled=True)
    return out.reshape(-1, cols)


def body(tokens, cotangent, expert_ids, gate_fixed, w_gate, w_up, w_down):
    experts = lax.axis_size("expert")
    n_blk = lax.axis_size("blk")
    rows, cols = tokens.shape
    ff = w_gate.shape[2]
    slots = experts * CAP
    chunk = slots // n_blk
    steps = ff // TILE
    goes_to = jnp.stack([block_at(d) for d in range(n_blk)])
    comes_from = jnp.stack([block_at((d // N_Y) * N_Y + (-d) % N_Y) for d in range(n_blk)])
    ids = expert_ids.T
    part = (chunk, ff)

    order = (3, 4, 1, 2, 5, 6, 7)

    def tiles(*block):
        zeros = (0,) * (len(block) - 1)
        return pl.BlockSpec(block, lambda i: zeros + (i,))

    def fixed(*block):
        zeros = (0,) * len(block)
        return pl.BlockSpec(block, lambda i: zeros)

    table = pl.BlockSpec(memory_space=pltpu.SMEM)
    (routed_x,) = call(route, [((slots, cols), BF16)], ids, tokens, limit=LARGE)
    arrived = to_experts(routed_x, experts)
    routed_cot, gate_hi, gate_lo = call(
        route_back,
        [((slots, cols + COUNT_LANES), BF16), ((rows, slots), BF16), ((rows, slots), BF16)],
        ids,
        gate_fixed.T,
        cotangent,
        limit=LARGE,
    )
    routed_cot, goes_to, comes_from = lax.optimization_barrier((routed_cot, goes_to, comes_from))
    span = 2 * TILE - NEAR
    shapes = [(N_Y, chunk, NEAR)] * 2 + [(2, chunk, span)] * N_Y
    far, near, *ups = call(
        project,
        [(a[:2] + (a[2] * steps,), BF16) for a in shapes],
        goes_to,
        arrived,
        w_gate[0],
        w_up[0],
        grid=(steps,),
        in_specs=[table, fixed(slots, cols), tiles(cols, TILE), tiles(cols, TILE)],
        out_specs=[tiles(*a) for a in shapes],
        scratch_shapes=[pltpu.VMEM((slots, cols), BF16)],
        limit=LARGE,
        flops=4 * slots * cols * ff,
        traffic=7_000_000,
    )
    arrived_cot = to_experts(routed_cot, experts)

    got_far = move(far, N_Y)
    got_ups = [ups[0]] + [move(ups[dy], dy) for dy in range(1, N_Y)]
    nears = call(meet_near, [((chunk, NEAR * steps), BF16)] * (N_Y - 1), near, got_far)
    (up_far,) = call(meet_far, [((chunk, span * steps), BF16)], *got_ups)
    got_nears = [move(g, dy) for dy, g in enumerate(nears, 1)]
    got_up = move(up_far, N_Y)
    *parts, loads = call(
        back,
        [((2,) + part, BF16)] * N_Y + [((8, COUNT_LANES), jnp.int32)],
        goes_to,
        arrived_cot,
        w_down[0],
        grid=(steps,),
        in_specs=[table, fixed(slots, cols + COUNT_LANES), pl.BlockSpec((TILE, cols), lambda i: (i, 0))],
        out_specs=[tiles(2, chunk, TILE)] * N_Y + [fixed(8, COUNT_LANES)],
        scratch_shapes=[pltpu.VMEM((slots, cols), BF16)],
        limit=LARGE,
        flops=2 * slots * cols * ff,
        traffic=4_000_000,
    )
    hidden, gate_pre, up_pre = call(
        activate,
        [((n_blk,) + part, BF16), (part, F32), (part, F32)],
        near,
        got_far,
        *got_nears,
        *got_ups,
        got_up,
    )
    hidden = lax.all_to_all(hidden, "blk", split_axis=0, concat_axis=0, tiled=True).reshape(slots, ff)
    got = [parts[0]] + [move(parts[dy], dy) for dy in range(1, N_Y)]
    (expert_out,) = call(
        expert,
        [((slots, cols), BF16)],
        w_down[0],
        hidden,
        limit=LARGE,
        flops=2 * slots * cols * ff,
        traffic=4_000_000,
    )
    returned = to_experts(expert_out, experts)
    (d_far,) = call(meet_far, [(part, BF16)], *got, flops=10**11)
    got_d = move(d_far, N_Y)
    d_gate, d_up = call(back_act, [(part, BF16)] * 2, gate_pre, up_pre, *got, got_d)
    got_du = [move(d_up, dy) for dy in range(1, N_Y)]
    got_dg = move(d_gate, N_Y)
    dg_pair = jnp.stack([d_gate, got_dg])
    du_four = jnp.stack([d_up] + got_du)
    dg = [dg_pair] + [move(dg_pair, dy) for dy in range(1, N_Y)]
    du = [du_four, move(du_four, N_Y)]
    (grad_down,) = call(
        grad_down_tile,
        [((ff, cols), BF16)],
        hidden,
        arrived_cot,
        grid=(steps,),
        in_specs=[pl.BlockSpec((slots, TILE), lambda i: (0, i)), fixed(slots, cols + COUNT_LANES)],
        out_specs=[pl.BlockSpec((TILE, cols), lambda i: (i, 0))],
        limit=LARGE,
        flops=2 * slots * cols * ff,
        traffic=4_000_000,
    )
    arrived, grad_down = lax.optimization_barrier((arrived, grad_down))
    (turned,) = call(
        turn,
        [((cols, slots), BF16)],
        comes_from,
        arrived,
        ordered=True,
        scratch_shapes=[pltpu.VMEM((slots, cols), BF16)],
    )
    (layer_out,) = call(combine, [((rows, cols), BF16)], gate_hi, gate_lo, returned)
    dg, du, grad_down, layer_out, turned = lax.optimization_barrier((dg, du, grad_down, layer_out, turned))
    grad_gate, grad_up = call(
        grad_tile,
        [((cols, ff), BF16)] * 2,
        turned,
        *dg,
        *du,
        grid=(steps,),
        in_specs=[fixed(cols, slots)] + [tiles(2, chunk, TILE)] * N_Y + [tiles(N_Y, chunk, TILE)] * 2,
        out_specs=[tiles(cols, TILE)] * 2,
        scratch_shapes=[pltpu.VMEM((slots, TILE), BF16)] * 2,
        flops=4 * slots * cols * ff,
        traffic=6_000_000,
    )
    return (layer_out, grad_gate[None], grad_up[None], grad_down[None], loads[:2].reshape(-1))


def solution(mesh):
    return jax.shard_map(
        body,
        mesh=mesh,
        in_specs=(
            P("expert", "blk"),
            P("expert", "blk"),
            P("expert", None),
            P("expert", None),
            P("expert", "blk", None),
            P("expert", "blk", None),
            P("expert", None, "blk"),
        ),
        out_specs=(
            P("expert", "blk"),
            P("expert", "blk", None),
            P("expert", "blk", None),
            P("expert", None, "blk"),
            P(),
        ),
        check_vma=False,
    )
```
